32 devices in a mesh: groups: 1, row: 32 (over z, y, x, core).
Axes of the slice: x: 2, y: 2, z: 4, core: 2. Of those that a mesh axis runs over, the one named last changes fastest.
Arguments:
- pair: bfloat16 [384, 384, 128], P(('groups', 'row')), may hold values from -6 to 6
- pair_mask: int32 [384, 384], P(('groups', 'row')), may hold values 0 or 1
- token_mask: int32 [384], P('groups'), may hold values 0 or 1
- proj_weights: bfloat16 [2, 128, 640], replicated, may hold values from -0.5 to 0.5
- out_weights: bfloat16 [2, 128, 128], replicated, may hold values from -0.5 to 0.5
Outputs:
- updated: bfloat16 [384, 384, 128], P(('groups', 'row'))
The draws below stay inside these ranges and needn't reach their ends.
All inputs are finite; a program needn't handle non-finite values. No bound on the sum of `pair_mask` on one device may be relied on, other than what follows from the above.
Results may differ from the reference program's by a relative error of at most 0.0075.
Values may be sent and summed in bfloat16 or wider, within the bound.
A program may use at most 64 MiB of HBM per device.

```python
import jax
import jax.numpy as jnp
from jax import lax

C = 128
CH = 128
TOKENS = 384


def set_ends(entries, own_key, low, high):
    place = [jax.random.randint(jax.random.fold_in(own_key, axis), (), 0, length) for axis, length in enumerate(entries.shape)]
    widest = entries.shape.index(max(entries.shape))
    beside = place[:widest] + [(place[widest] + 1) % entries.shape[widest]] + place[widest + 1:]
    return entries.at[tuple(place)].set(low).at[tuple(beside)].set(high)


def levels(key, extent, shards, least, top_value):
    def one(dim, shards_of):
        steps = jax.random.uniform(jax.random.fold_in(jax.random.fold_in(key, 6), dim), (shards_of,), jnp.float32, least / len(shards), top_value / len(shards))
        return jnp.repeat(jnp.exp(steps), extent[dim] // shards_of).reshape((-1,) + (1,) * (len(extent) - dim - 1))

    factor_of = one(*shards[0])
    for cut in shards[1:]:
        factor_of = factor_of * one(*cut)
    return factor_of


def scatter_about(own_key, dims, scale, reach, cuts=(), dtype=jnp.bfloat16):
    result = scale * jax.random.normal(own_key, dims, jnp.float32)
    if cuts:
        result = result * levels(own_key, dims, cuts, -0.22, 0.18)
    return jnp.clip(result, -reach, reach).astype(dtype)


def setup_inputs(seed: int = 0, part: int = 0) -> dict:
    key_of = jax.random.split(jax.random.key(seed), 6)
    part_splits = jax.random.split(jax.random.fold_in(key_of[5], part), 6)
    pair = scatter_about(part_splits[0], (TOKENS, TOKENS, C), 1.0, 6.0, ((0, 32),))
    pair_mask = set_ends((jax.random.randint(part_splits[1], (TOKENS, TOKENS), 0, 8) < 7).astype(jnp.int32), jax.random.fold_in(part_splits[1], 1), 0, 1)
    token_mask = set_ends((jax.random.randint(part_splits[2], (TOKENS,), 0, 16) < 15).astype(jnp.int32), jax.random.fold_in(part_splits[2], 1), 0, 1)
    proj_weights = scatter_about(key_of[3], (2, C, 4 * CH + C), C ** -0.5, 0.5)
    out_weights = scatter_about(key_of[4], (2, CH, C), CH ** -0.5, 0.5)
    return dict(pair=pair, pair_mask=pair_mask, token_mask=token_mask, proj_weights=proj_weights, out_weights=out_weights)


EPS = 1e-05

def norm_axis(values, axis):
    mean = lax.optimization_barrier(jnp.mean(values, axis=axis, keepdims=True))
    centred = values - mean
    var = lax.optimization_barrier(jnp.mean(centred * centred, axis=axis, keepdims=True))
    return centred * lax.rsqrt(var + EPS)

def triangle_update(state, weights, out_w, mask, incoming):
    width = out_w.shape[0]
    normed = norm_axis(state.astype(jnp.float32), -1).astype(jnp.bfloat16)
    normed_f = normed.astype(jnp.float32)
    weights_f = weights.astype(jnp.float32)

    def channel_major(lo):
        return jnp.einsum('ijc,cd->dij', normed_f, weights_f[:, lo:lo + width])
    left = (mask[None] * jax.nn.sigmoid(channel_major(0)) * channel_major(width)).astype(jnp.bfloat16)
    right = (mask[None] * jax.nn.sigmoid(channel_major(2 * width)) * channel_major(3 * width)).astype(jnp.bfloat16)
    gate = jax.nn.sigmoid(jnp.einsum('ijc,cd->ijd', normed_f, weights_f[:, 4 * width:]))

    def per_channel(pieces):
        left_c, right_c = pieces
        if incoming:
            return jnp.dot(left_c.T, right_c, preferred_element_type=jnp.float32)
        return jnp.dot(left_c, right_c.T, preferred_element_type=jnp.float32)
    tri = lax.map(per_channel, (left, right)).astype(jnp.bfloat16)
    tri_normed = norm_axis(tri.astype(jnp.float32), 0).astype(jnp.bfloat16)
    out = jnp.einsum('cij,cd->ijd', tri_normed.astype(jnp.float32), out_w.astype(jnp.float32))
    return (state.astype(jnp.float32) + gate * out).astype(jnp.bfloat16)

def reference(pair, pair_mask, token_mask, proj_weights, out_weights):
    tok = token_mask.astype(jnp.float32)
    mask = pair_mask.astype(jnp.float32) * tok[:, None] * tok[None, :]
    state = triangle_update(pair, proj_weights[0], out_weights[0], mask, False)
    state = triangle_update(state, proj_weights[1], out_weights[1], mask, True)
    return state
```

```python
import functools

import jax
import jax.numpy as jnp
from jax import lax
from jax.experimental import pallas as pl
from jax.experimental.pallas import tpu as pltpu
from jax.sharding import PartitionSpec as P

EPS = 1e-05
MESH = pl.DeviceIdType.MESH


def norm_axis(values, axis):
    mean = jnp.mean(values, axis=axis, keepdims=True)
    centred = values - mean
    var = jnp.mean(centred * centred, axis=axis, keepdims=True)
    return centred * lax.rsqrt(var + EPS)


def dot(a, b, dims):
    return lax.dot_general(a, b, (dims, ((), ())), preferred_element_type=jnp.float32)


def exchange_kernel(n, kinds, *refs):
    m = len(kinds)
    srcs, outs = refs[:m], refs[m : 2 * m]
    send_sem, recv_sem, own_sem = refs[2 * m :]
    h = n // 2
    g = lax.axis_index("groups")
    me = lax.axis_index("row")
    half, q, core = me // h, me % h, me % 2
    wide = any(kind != "half" for kind in kinds)
    barrier = pltpu.get_barrier_semaphore()

    def greet(base, s):
        pl.semaphore_signal(
            barrier, inc=1, device_id=(g, base * h + (q + s) % h), device_id_type=MESH
        )

    def greet_near(s, carry):
        greet(half, s)
        return carry

    def greet_far(s, carry):
        greet(1 - half, s)
        return carry

    lax.fori_loop(1, h, greet_near, 0)
    if wide:
        lax.fori_loop(0, h, greet_far, 0)
    pl.semaphore_wait(barrier, (n if wide else h) - 1)

    def send(i, block, slot, dest):
        pltpu.make_async_remote_copy(
            src_ref=srcs[i].at[block],
            dst_ref=outs[i].at[slot],
            send_sem=send_sem.at[i],
            recv_sem=recv_sem.at[i],
            device_id=(g, dest),
            device_id_type=MESH,
        ).start()

    def far(to):
        dest = (1 - half) * h + to
        for i, kind in enumerate(kinds):
            if kind != "half":
                send(i, to if kind == "both" else dest, me, dest)

    def near(to):
        dest = half * h + to

        @pl.when(to != q)
        def _():
            for i, kind in enumerate(kinds):
                send(i, dest if kind == "all" else to, q if kind == "half" else me, dest)

    def step(s, carry):
        to = (q + s) % h if h & (h - 1) else q ^ s ^ (core * (h - 2))
        if wide:
            far(to)
        near(to)
        return carry

    lax.fori_loop(0, h, step, 0)
    own = []
    for i, kind in enumerate(kinds):
        copy = pltpu.make_async_copy(
            srcs[i].at[me if kind == "all" else q],
            outs[i].at[q if kind == "half" else me],
            own_sem.at[i],
        )
        copy.start()
        own.append(copy)
    for copy in own:
        copy.wait()
    for i, kind in enumerate(kinds):
        got = outs[i].at[pl.ds(0, (h if kind == "half" else n) - 1)]
        pltpu.make_async_copy(got, got, recv_sem.at[i]).wait()
        pltpu.make_async_copy(got, got, send_sem.at[i]).wait()


def exchange(n, kinds, ident, *srcs):
    m = len(kinds)
    shapes = [
        jax.ShapeDtypeStruct((n // 2 if kind == "half" else n,) + src.shape[1:], src.dtype)
        for kind, src in zip(kinds, srcs)
    ]
    return pl.pallas_call(
        functools.partial(exchange_kernel, n, kinds),
        out_shape=shapes,
        in_specs=[pl.BlockSpec(memory_space=pl.ANY)] * m,
        out_specs=[pl.BlockSpec(memory_space=pl.ANY)] * m,
        scratch_shapes=[pltpu.SemaphoreType.DMA((m,))] * 3,
        compiler_params=pltpu.CompilerParams(collective_id=ident, has_side_effects=True),
    )(*srcs)


def normed_row(state_ref, r):
    return norm_axis(state_ref[r].astype(jnp.float32), -1).astype(jnp.bfloat16)


def project_row(normed, w_ref, mask_ref, left_ref, right_ref, r):
    owners, _, share, _ = left_ref.shape
    width = owners * share
    mask = mask_ref[pl.ds(r, 1), :]
    for lo, out_ref in ((0, left_ref), (2 * width, right_ref)):
        proj = dot(w_ref[:, lo : lo + 2 * width], normed, ((0,), (1,)))
        side = (mask * jax.nn.sigmoid(proj[:width]) * proj[width:]).astype(out_ref.dtype)
        for owner in range(owners):
            out_ref[owner, r] = side[owner * share : (owner + 1) * share]


def finish_row(state_ref, normed, w_ref, wo_ref, tri_ref, r):
    sources, _, share, tokens = tri_ref.shape
    width = wo_ref.shape[0]
    owners = width // share
    tri = jnp.concatenate([tri_ref[s, r].astype(jnp.float32) for s in range(owners)], axis=0)
    if sources > owners:
        tri += jnp.concatenate(
            [tri_ref[s, r].astype(jnp.float32) for s in range(owners, sources)], axis=0
        )
    tri_normed = norm_axis(tri, 0).astype(jnp.bfloat16)
    out = dot(tri_normed, wo_ref[...], ((0,), (0,)))
    gate = jax.nn.sigmoid(dot(normed, w_ref[:, 4 * width :], ((1,), (0,))))
    return (state_ref[r].astype(jnp.float32) + gate * out).astype(jnp.bfloat16)


def first_kernel(state_ref, mask_ref, w_ref, left_ref, right_ref):
    def row(r, carry):
        project_row(normed_row(state_ref, r), w_ref, mask_ref, left_ref, right_ref, r)
        return carry

    lax.fori_loop(0, state_ref.shape[0], row, 0)


def middle_kernel(
    state_ref, mask_ref, w_ref, wo_ref, w_next_ref, tri_ref, next_ref, left_ref, right_ref
):
    def row(r, carry):
        next_ref[r] = finish_row(
            state_ref, normed_row(state_ref, r), w_ref, wo_ref, tri_ref, r
        )
        project_row(normed_row(next_ref, r), w_next_ref, mask_ref, left_ref, right_ref, r)
        return carry

    lax.fori_loop(0, state_ref.shape[0], row, 0)


def last_kernel(state_ref, w_ref, wo_ref, tri_ref, next_ref):
    def row(r, carry):
        next_ref[r] = finish_row(
            state_ref, normed_row(state_ref, r), w_ref, wo_ref, tri_ref, r
        )
        return carry

    lax.fori_loop(0, state_ref.shape[0], row, 0)


def local(body, out_shape, *args):
    vmem = pl.BlockSpec(memory_space=pltpu.VMEM)
    return pl.pallas_call(
        body,
        out_shape=out_shape,
        in_specs=[vmem] * len(args),
        out_specs=jax.tree.map(lambda _: vmem, out_shape),
        compiler_params=pltpu.CompilerParams(vmem_limit_bytes=40 * 2**20),
    )(*args)


def on_device(pair, pair_mask, token_mask, proj_weights, out_weights):
    rows, tokens, _ = pair.shape
    n = lax.axis_size("row")
    h = n // 2
    share = out_weights.shape[1] // h
    offset = lax.axis_index("row") * rows
    tok_rows = lax.dynamic_slice_in_dim(token_mask, offset, rows).astype(jnp.float32)
    tok_cols = token_mask.astype(jnp.float32)
    mask = pair_mask.astype(jnp.float32) * tok_rows[:, None] * tok_cols[None, :]
    side = jax.ShapeDtypeStruct((h, rows, share, tokens), jnp.bfloat16)
    state_shape = jax.ShapeDtypeStruct(pair.shape, pair.dtype)

    left, right = local(first_kernel, [side, side], pair, mask, proj_weights[0])
    left, right = exchange(n, ("half", "both"), 1, left, right)
    tri = jnp.einsum("srck,tuck->srctu", left, right, preferred_element_type=jnp.float32)
    tri = tri.astype(jnp.bfloat16).reshape(h, rows, share, tokens)
    (tri,) = exchange(n, ("half",), 2, tri)
    state, left, right = local(
        middle_kernel,
        [state_shape, side, side],
        pair,
        mask,
        proj_weights[0],
        out_weights[0],
        proj_weights[1],
        tri,
    )
    left, right = exchange(n, ("half", "half"), 3, left, right)
    tri = jnp.einsum("srci,srcj->icj", left, right, preferred_element_type=jnp.float32)
    tri = tri.astype(jnp.bfloat16).reshape(n, rows, share, tokens)
    (tri,) = exchange(n, ("all",), 4, tri)
    return local(last_kernel, state_shape, state, proj_weights[1], out_weights[1], tri)


def solution(mesh):
    return jax.shard_map(
        on_device,
        mesh=mesh,
        in_specs=(
            P(("groups", "row"), None, None),
            P(("groups", "row"), None),
            P("groups"),
            P(),
            P(),
        ),
        out_specs=P(("groups", "row"), None, None),
        check_vma=False,
    )
```

```python
import functools

import jax
import jax.numpy as jnp
from jax import lax
from jax.experimental import pallas as pl
from jax.experimental.pallas import tpu as pltpu
from jax.sharding import PartitionSpec as P

EPS = 1e-05
MESH = pl.DeviceIdType.MESH


def norm_axis(values, axis):
    mean = jnp.mean(values, axis=axis, keepdims=True)
    centred = values - mean
    var = jnp.mean(centred * centred, axis=axis, keepdims=True)
    return centred * lax.rsqrt(var + EPS)


def dot(a, b, dims):
    return lax.dot_general(a, b, (dims, ((), ())), preferred_element_type=jnp.float32)


def exchange_kernel(n, kinds, *refs):
    m = len(kinds)
    srcs, outs = refs[:m], refs[m : 2 * m]
    send_sem, recv_sem, own_sem = refs[2 * m :]
    h = n // 2
    g = lax.axis_index("groups")
    me = lax.axis_index("row")
    half, q, core = me // h, me % h, me % 2
    wide = any(kind != "half" for kind in kinds)
    barrier = pltpu.get_barrier_semaphore()

    def greet(base, s):
        pl.semaphore_signal(
            barrier, inc=1, device_id=(g, base * h + (q + s) % h), device_id_type=MESH
        )

    def greet_near(s, carry):
        greet(half, s)
        return carry

    def greet_far(s, carry):
        greet(1 - half, s)
        return carry

    lax.fori_loop(1, h, greet_near, 0)
    if wide:
        lax.fori_loop(0, h, greet_far, 0)
    pl.semaphore_wait(barrier, (n if wide else h) - 1)

    def send(i, block, slot, dest):
        pltpu.make_async_remote_copy(
            src_ref=srcs[i].at[block],
            dst_ref=outs[i].at[slot],
            send_sem=send_sem.at[i],
            recv_sem=recv_sem.at[i],
            device_id=(g, dest),
            device_id_type=MESH,
        ).start()

    def far(to):
        dest = (1 - half) * h + to
        for i, kind in enumerate(kinds):
            if kind != "half":
                send(i, to if kind == "both" else dest, me, dest)

    def near(to):
        dest = half * h + to

        @pl.when(to != q)
        def _():
            for i, kind in enumerate(kinds):
                send(i, dest if kind == "all" else to, q if kind == "half" else me, dest)

    def step(s, carry):
        to = (q + s) % h if h & (h - 1) else q ^ s ^ (core * (h - 2))
        if wide:
            far(to)
        near(to)
        return carry

    lax.fori_loop(0, h, step, 0)
    own = []
    for i, kind in enumerate(kinds):
        copy = pltpu.make_async_copy(
            srcs[i].at[me if kind == "all" else q],
            outs[i].at[q if kind == "half" else me],
            own_sem.at[i],
        )
        copy.start()
        own.append(copy)
    for copy in own:
        copy.wait()
    for i, kind in enumerate(kinds):
        got = outs[i].at[pl.ds(0, (h if kind == "half" else n) - 1)]
        pltpu.make_async_copy(got, got, recv_sem.at[i]).wait()
        pltpu.make_async_copy(got, got, send_sem.at[i]).wait()


def exchange(n, kinds, ident, *srcs):
    m = len(kinds)
    shapes = [
        jax.ShapeDtypeStruct((n // 2 if kind == "half" else n,) + src.shape[1:], src.dtype)
        for kind, src in zip(kinds, srcs)
    ]
    return pl.pallas_call(
        functools.partial(exchange_kernel, n, kinds),
        out_shape=shapes,
        in_specs=[pl.BlockSpec(memory_space=pltpu.VMEM)] * m,
        out_specs=[pl.BlockSpec(memory_space=pltpu.VMEM)] * m,
        scratch_shapes=[pltpu.SemaphoreType.DMA((m,))] * 3,
        compiler_params=pltpu.CompilerParams(collective_id=ident, has_side_effects=True),
    )(*srcs)


def normed_row(state_ref, r):
    return norm_axis(state_ref[r].astype(jnp.float32), -1).astype(jnp.bfloat16)


def project_row(normed, w_ref, mask_ref, left_ref, right_ref, r):
    owners, _, share, _ = left_ref.shape
    width = owners * share
    mask = mask_ref[pl.ds(r, 1), :]
    for lo, out_ref in ((0, left_ref), (2 * width, right_ref)):
        proj = dot(w_ref[:, lo : lo + 2 * width], normed, ((0,), (1,)))
        side = (mask * jax.nn.sigmoid(proj[:width]) * proj[width:]).astype(out_ref.dtype)
        for owner in range(owners):
            out_ref[owner, r] = side[owner * share : (owner + 1) * share]


def finish_row(state_ref, normed, w_ref, wo_ref, tri_ref, r):
    sources, _, share, tokens = tri_ref.shape
    width = wo_ref.shape[0]
    owners = width // share
    tri = jnp.concatenate([tri_ref[s, r].astype(jnp.float32) for s in range(owners)], axis=0)
    if sources > owners:
        tri += jnp.concatenate(
            [tri_ref[s, r].astype(jnp.float32) for s in range(owners, sources)], axis=0
        )
    tri_normed = norm_axis(tri, 0).astype(jnp.bfloat16)
    out = dot(tri_normed, wo_ref[...], ((0,), (0,)))
    gate = jax.nn.sigmoid(dot(normed, w_ref[:, 4 * width :], ((1,), (0,))))
    return (state_ref[r].astype(jnp.float32) + gate * out).astype(jnp.bfloat16)


def first_kernel(state_ref, mask_ref, w_ref, left_ref, right_ref):
    def row(r, carry):
        project_row(normed_row(state_ref, r), w_ref, mask_ref, left_ref, right_ref, r)
        return carry

    lax.fori_loop(0, state_ref.shape[0], row, 0)


def middle_kernel(
    state_ref, mask_ref, w_ref, wo_ref, w_next_ref, tri_ref, next_ref, left_ref, right_ref
):
    def row(r, carry):
        next_ref[r] = finish_row(
            state_ref, normed_row(state_ref, r), w_ref, wo_ref, tri_ref, r
        )
        project_row(normed_row(next_ref, r), w_next_ref, mask_ref, left_ref, right_ref, r)
        return carry

    lax.fori_loop(0, state_ref.shape[0], row, 0)


def last_kernel(state_ref, w_ref, wo_ref, tri_ref, next_ref):
    def row(r, carry):
        next_ref[r] = finish_row(
            state_ref, normed_row(state_ref, r), w_ref, wo_ref, tri_ref, r
        )
        return carry

    lax.fori_loop(0, state_ref.shape[0], row, 0)


def local(body, out_shape, *args):
    vmem = pl.BlockSpec(memory_space=pltpu.VMEM)
    return pl.pallas_call(
        body,
        out_shape=out_shape,
        in_specs=[vmem] * len(args),
        out_specs=jax.tree.map(lambda _: vmem, out_shape),
        compiler_params=pltpu.CompilerParams(vmem_limit_bytes=40 * 2**20),
    )(*args)


def on_device(pair, pair_mask, token_mask, proj_weights, out_weights):
    rows, tokens, _ = pair.shape
    n = lax.axis_size("row")
    h = n // 2
    share = out_weights.shape[1] // h
    offset = lax.axis_index("row") * rows
    tok_rows = lax.dynamic_slice_in_dim(token_mask, offset, rows).astype(jnp.float32)
    tok_cols = token_mask.astype(jnp.float32)
    mask = pair_mask.astype(jnp.float32) * tok_rows[:, None] * tok_cols[None, :]
    side = jax.ShapeDtypeStruct((h, rows, share, tokens), jnp.bfloat16)
    state_shape = jax.ShapeDtypeStruct(pair.shape, pair.dtype)

    left, right = local(first_kernel, [side, side], pair, mask, proj_weights[0])
    left, right = exchange(n, ("half", "both"), 1, left, right)
    left = left.reshape(h * rows, share, tokens)
    right = right.reshape(tokens, share, tokens)
    tri = jnp.einsum("ick,jck->icj", left, right, preferred_element_type=jnp.float32)
    tri = tri.astype(jnp.bfloat16).reshape(h, rows, share, tokens)
    (tri,) = exchange(n, ("half",), 2, tri)
    state, left, right = local(
        middle_kernel,
        [state_shape, side, side],
        pair,
        mask,
        proj_weights[0],
        out_weights[0],
        proj_weights[1],
        tri,
    )
    left, right = exchange(n, ("half", "half"), 3, left, right)
    tri = jnp.einsum("srci,srcj->icj", left, right, preferred_element_type=jnp.float32)
    tri = tri.astype(jnp.bfloat16).reshape(n, rows, share, tokens)
    (tri,) = exchange(n, ("all",), 4, tri)
    return local(last_kernel, state_shape, state, proj_weights[1], out_weights[1], tri)


def solution(mesh):
    return jax.shard_map(
        on_device,
        mesh=mesh,
        in_specs=(
            P(("groups", "row"), None, None),
            P(("groups", "row"), None),
            P("groups"),
            P(),
            P(),
        ),
        out_specs=P(("groups", "row"), None, None),
        check_vma=False,
    )
```

```python
import functools

import jax
import jax.numpy as jnp
from jax import lax
from jax.experimental import pallas as pl
from jax.experimental.pallas import tpu as pltpu
from jax.sharding import PartitionSpec as P

EPS = 1e-05
MESH = pl.DeviceIdType.MESH


def norm_axis(values, axis):
    mean = jnp.mean(values, axis=axis, keepdims=True)
    centred = values - mean
    var = jnp.mean(centred * centred, axis=axis, keepdims=True)
    return centred * lax.rsqrt(var + EPS)


def dot(a, b, dims):
    return lax.dot_general(a, b, (dims, ((), ())), preferred_element_type=jnp.float32)


class Net:
    def __init__(self, n, wide):
        self.n, self.h, self.wide = n, n // 2, wide
        self.g = lax.axis_index("groups")
        self.me = lax.axis_index("row")
        self.half, self.q, self.core = self.me // self.h, self.me % self.h, self.me % 2

    def greet(self):
        barrier = pltpu.get_barrier_semaphore()

        def signal(dest):
            pl.semaphore_signal(
                barrier, inc=1, device_id=(self.g, dest), device_id_type=MESH
            )

        def near(s, carry):
            signal(self.half * self.h + (self.q + s) % self.h)
            return carry

        def far(s, carry):
            signal((1 - self.half) * self.h + (self.q + s) % self.h)
            return carry

        lax.fori_loop(1, self.h, near, 0)
        if self.wide:
            lax.fori_loop(0, self.h, far, 0)

    def met(self):
        pl.semaphore_wait(pltpu.get_barrier_semaphore(), (self.n if self.wide else self.h) - 1)


class Swap:
    def __init__(self, net, kind, src, dst, sems, step):
        self.net, self.kind, self.src, self.dst, self.step = net, kind, src, dst, step
        self.send_sem, self.recv_sem, self.own_sem = sems
        self.slot = net.q if kind == "half" else net.me
        self.count = net.h if kind == "half" else net.n

    def rows(self, t):
        return pl.ds(t * self.step, self.step)

    def block(self, to, dest):
        return dest if self.kind == "all" else to

    def send(self, t, to, dest):
        pltpu.make_async_remote_copy(
            src_ref=self.src.at[self.block(to, dest), self.rows(t)],
            dst_ref=self.dst.at[self.slot, self.rows(t)],
            send_sem=self.send_sem,
            recv_sem=self.recv_sem.at[t],
            device_id=(self.net.g, dest),
            device_id_type=MESH,
        ).start()

    def own(self, t):
        net = self.net
        return pltpu.make_async_copy(
            self.src.at[self.block(net.q, net.me), self.rows(t)],
            self.dst.at[self.slot, self.rows(t)],
            self.own_sem.at[t],
        )

    def arrived(self, t):
        self.own(t).wait()
        got = self.dst.at[pl.ds(0, self.count - 1), self.rows(t)]
        pltpu.make_async_copy(got, got, self.recv_sem.at[t]).wait()

    def sent(self):
        gone = self.dst.at[pl.ds(0, self.count - 1)]
        pltpu.make_async_copy(gone, gone, self.send_sem).wait()


def send_rows(net, swaps, t):
    h = net.h

    def step(s, carry):
        to = (net.q + s) % h if h & (h - 1) else net.q ^ s ^ (net.core * (h - 2))
        for swap in swaps:
            if swap.kind != "half":
                swap.send(t, to, (1 - net.half) * h + to)

        @pl.when(to != net.q)
        def _():
            for swap in swaps:
                swap.send(t, to, net.half * h + to)

        return carry

    for swap in swaps:
        swap.own(t).start()
    lax.fori_loop(0, h, step, 0)


def normed_row(state_ref, r):
    return norm_axis(state_ref[r].astype(jnp.float32), -1).astype(jnp.bfloat16)


def project_row(normed, u, w_ref, pair_mask_ref, token_mask_ref, left_ref, right_ref, r):
    owners, rows, share, tokens = left_ref.shape
    width = owners * share
    token = lax.axis_index("row") * rows + r
    columns = token_mask_ref[...]
    here = lax.broadcasted_iota(jnp.int32, (1, tokens), 1) == token
    row_token = jnp.sum(jnp.where(here, columns, 0.0), axis=1, keepdims=True)
    mask = pair_mask_ref[pl.ds(r, 1), :].astype(jnp.float32) * row_token * columns
    for lo, out_ref in ((0, left_ref), (2 * width, right_ref)):
        proj = dot(w_ref[u, :, lo : lo + 2 * width], normed, ((0,), (1,)))
        side = (mask * jax.nn.sigmoid(proj[:width]) * proj[width:]).astype(out_ref.dtype)
        for owner in range(owners):
            out_ref[owner, r] = side[owner * share : (owner + 1) * share]


def finish_row(state_ref, u, w_ref, wo_ref, tri_ref, r):
    sources, _, share, _ = tri_ref.shape
    width = wo_ref.shape[1]
    owners = width // share
    normed = normed_row(state_ref, r)
    tri = jnp.concatenate([tri_ref[s, r].astype(jnp.float32) for s in range(owners)], axis=0)
    if sources > owners:
        tri += jnp.concatenate(
            [tri_ref[s, r].astype(jnp.float32) for s in range(owners, sources)], axis=0
        )
    tri_normed = norm_axis(tri, 0).astype(jnp.bfloat16)
    out = dot(tri_normed, wo_ref[u], ((0,), (0,)))
    gate = jax.nn.sigmoid(dot(normed, w_ref[u, :, 4 * width :], ((1,), (0,))))
    return (state_ref[r].astype(jnp.float32) + gate * out).astype(jnp.bfloat16)


def each_row(t, step, body):
    def row(r, carry):
        body(r)
        return carry

    lax.fori_loop(t * step, (t + 1) * step, row, 0)


def first_kernel(n, step, state, pair_mask, token_mask, w, left, right, left_src, right_src, *sems):
    net = Net(n, True)
    swaps = [
        Swap(net, "half", left_src, left, sems[:3], step),
        Swap(net, "both", right_src, right, sems[3:], step),
    ]
    parts = state.shape[0] // step
    net.greet()
    for t in range(parts):
        each_row(
            t,
            step,
            lambda r: project_row(
                normed_row(state, r), 0, w, pair_mask, token_mask, left_src, right_src, r
            ),
        )
        if t == 0:
            net.met()
        send_rows(net, swaps, t)
    for swap in swaps:
        for t in range(parts):
            swap.arrived(t)
        swap.sent()


def middle_kernel(
    n, step, state, pair_mask, token_mask, w, wo, tri_src, after, left, right, tri, left_src, right_src, *sems
):
    net = Net(n, False)
    tri_swap = Swap(net, "half", tri_src, tri, sems[:3], step)
    swaps = [
        Swap(net, "half", left_src, left, sems[3:6], step),
        Swap(net, "half", right_src, right, sems[6:], step),
    ]
    parts = state.shape[0] // step
    net.greet()
    net.met()
    for t in range(parts):
        send_rows(net, [tri_swap], t)

    def body(r):
        after[r] = finish_row(state, 0, w, wo, tri, r)
        project_row(normed_row(after, r), 1, w, pair_mask, token_mask, left_src, right_src, r)

    for t in range(parts):
        tri_swap.arrived(t)
        each_row(t, step, body)
        send_rows(net, swaps, t)
    tri_swap.sent()
    for swap in swaps:
        for t in range(parts):
            swap.arrived(t)
        swap.sent()


def last_kernel(n, step, state, w, wo, tri_src, after, tri, *sems):
    net = Net(n, True)
    swap = Swap(net, "all", tri_src, tri, sems, step)
    parts = state.shape[0] // step
    net.greet()
    net.met()
    for t in range(parts):
        send_rows(net, [swap], t)

    def body(r):
        after[r] = finish_row(state, 1, w, wo, tri, r)

    for t in range(parts):
        swap.arrived(t)
        each_row(t, step, body)
    swap.sent()


def call(body, ident, n, step, swaps, args, outs, scratch):
    vmem = pl.BlockSpec(memory_space=pltpu.VMEM)
    parts = args[0].shape[0] // step
    dma = pltpu.SemaphoreType.DMA
    return pl.pallas_call(
        functools.partial(body, n, step),
        out_shape=[jax.ShapeDtypeStruct(shape, jnp.bfloat16) for shape in outs],
        in_specs=[vmem] * len(args),
        out_specs=[vmem] * len(outs),
        scratch_shapes=[pltpu.VMEM(shape, jnp.bfloat16) for shape in scratch]
        + [dma, dma((parts,)), dma((parts,))] * swaps,
        compiler_params=pltpu.CompilerParams(
            collective_id=ident, has_side_effects=True, vmem_limit_bytes=28 * 2**20
        ),
    )(*args)


def on_device(pair, pair_mask, token_mask, w, wo):
    rows, tokens, _ = pair.shape
    n = lax.axis_size("row")
    h = n // 2
    share = wo.shape[1] // h
    step = 4 if rows % 4 == 0 else rows
    cols = token_mask.astype(jnp.float32)[None, :]
    near, full = (h, rows, share, tokens), (n, rows, share, tokens)

    left, right = call(
        first_kernel, 1, n, step, 2, (pair, pair_mask, cols, w), (near, full), (near, near)
    )
    left = left.reshape(h * rows, share, tokens)
    right = right.reshape(tokens, share, tokens)
    tri = jnp.einsum("ick,jck->icj", left, right, preferred_element_type=jnp.float32)
    tri = tri.astype(jnp.bfloat16).reshape(near)
    state, left, right = call(
        middle_kernel,
        2,
        n,
        step,
        3,
        (pair, pair_mask, cols, w, wo, tri),
        (pair.shape, near, near),
        (near, near, near),
    )
    left = left.reshape(h * rows, share, tokens)
    right = right.reshape(h * rows, share, tokens)
    tri = jnp.einsum("kci,kcj->icj", left, right, preferred_element_type=jnp.float32)
    tri = tri.astype(jnp.bfloat16).reshape(full)
    return call(last_kernel, 3, n, step, 1, (state, w, wo, tri), (pair.shape,), (full,))[0]


def solution(mesh):
    return jax.shard_map(
        on_device,
        mesh=mesh,
        in_specs=(
            P(("groups", "row"), None, None),
            P(("groups", "row"), None),
            P("groups"),
            P(),
            P(),
        ),
        out_specs=P(("groups", "row"), None, None),
        check_vma=False,
    )
```

```python
import functools

import jax
import jax.numpy as jnp
from jax import lax
from jax.experimental import pallas as pl
from jax.experimental.pallas import tpu as pltpu
from jax.sharding import PartitionSpec as P

EPS = 1e-05
MESH = pl.DeviceIdType.MESH
FIRST, MIDDLE, LAST = (4, 4, 4), (1, 1, 2, 2, 3, 3), (6, 4, 2)


def norm_axis(values, axis):
    mean = jnp.mean(values, axis=axis, keepdims=True)
    centred = values - mean
    var = jnp.mean(centred * centred, axis=axis, keepdims=True)
    return centred * lax.rsqrt(var + EPS)


def dot(a, b, dims):
    return lax.dot_general(a, b, (dims, ((), ())), preferred_element_type=jnp.float32)


def cut(rows, sizes):
    if sum(sizes) != rows:
        return ((0, rows),)
    return tuple((sum(sizes[:t]), size) for t, size in enumerate(sizes))


class Net:
    def __init__(self, n, wide):
        self.n, self.h, self.wide = n, n // 2, wide
        self.g = lax.axis_index("groups")
        self.me = lax.axis_index("row")
        self.half, self.q, self.core = self.me // self.h, self.me % self.h, self.me % 2

    def greet(self):
        barrier = pltpu.get_barrier_semaphore()

        def signal(dest):
            pl.semaphore_signal(
                barrier, inc=1, device_id=(self.g, dest), device_id_type=MESH
            )

        def near(s, carry):
            signal(self.half * self.h + (self.q + s) % self.h)
            return carry

        def far(s, carry):
            signal((1 - self.half) * self.h + (self.q + s) % self.h)
            return carry

        lax.fori_loop(1, self.h, near, 0)
        if self.wide:
            lax.fori_loop(0, self.h, far, 0)

    def met(self):
        pl.semaphore_wait(pltpu.get_barrier_semaphore(), (self.n if self.wide else self.h) - 1)


class Swap:
    def __init__(self, net, kind, src, dst, sems, parts):
        self.net, self.kind, self.src, self.dst, self.parts = net, kind, src, dst, parts
        self.send_sem, self.recv_sem, self.own_sem = sems
        self.slot = net.q if kind == "half" else net.me
        self.count = net.h if kind == "half" else net.n

    def rows(self, t):
        return pl.ds(*self.parts[t])

    def block(self, to, dest):
        return dest if self.kind == "all" else to

    def send(self, t, to, dest):
        pltpu.make_async_remote_copy(
            src_ref=self.src.at[self.block(to, dest), self.rows(t)],
            dst_ref=self.dst.at[self.slot, self.rows(t)],
            send_sem=self.send_sem,
            recv_sem=self.recv_sem.at[t],
            device_id=(self.net.g, dest),
            device_id_type=MESH,
        ).start()

    def own(self, t):
        net = self.net
        return pltpu.make_async_copy(
            self.src.at[self.block(net.q, net.me), self.rows(t)],
            self.dst.at[self.slot, self.rows(t)],
            self.own_sem.at[t],
        )

    def arrived(self, t):
        self.own(t).wait()
        got = self.dst.at[pl.ds(0, self.count - 1), self.rows(t)]
        pltpu.make_async_copy(got, got, self.recv_sem.at[t]).wait()

    def sent(self):
        gone = self.dst.at[pl.ds(0, self.count - 1)]
        pltpu.make_async_copy(gone, gone, self.send_sem).wait()


def send_rows(net, swaps, t):
    h = net.h

    def step(s, carry):
        to = (net.q + s) % h if h & (h - 1) else net.q ^ s ^ (net.core * (h - 2))
        for swap in swaps:
            if swap.kind != "half":
                swap.send(t, to, (1 - net.half) * h + to)

        @pl.when(to != net.q)
        def _():
            for swap in swaps:
                swap.send(t, to, net.half * h + to)

        return carry

    for swap in swaps:
        swap.own(t).start()
    lax.fori_loop(0, h, step, 0)


def normed_row(state_ref, r):
    return norm_axis(state_ref[r].astype(jnp.float32), -1).astype(jnp.bfloat16)


def mask_row(pair_mask_ref, token_mask_ref, r):
    rows, tokens = pair_mask_ref.shape
    token = lax.axis_index("row") * rows + r
    columns = token_mask_ref[...].astype(jnp.float32)
    here = lax.broadcasted_iota(jnp.int32, (1, tokens), 1) == token
    row_token = jnp.sum(jnp.where(here, columns, 0.0), axis=1, keepdims=True)
    return pair_mask_ref[pl.ds(r, 1), :].astype(jnp.float32) * row_token * columns


def project_row(normed, w, mask, out_ref, r):
    owners, _, share, _ = out_ref.shape
    proj = dot(w, normed, ((0,), (1,)))
    half = owners * share
    side = (mask * jax.nn.sigmoid(proj[:half]) * proj[half:]).astype(out_ref.dtype)
    for owner in range(owners):
        out_ref[owner, r] = side[owner * share : (owner + 1) * share]


def finish_row(state_ref, u, w_ref, wo_ref, tri_ref, r):
    sources, _, share, _ = tri_ref.shape
    width = wo_ref.shape[1]
    owners = width // share
    normed = normed_row(state_ref, r)
    tri = jnp.concatenate([tri_ref[s, r].astype(jnp.float32) for s in range(owners)], axis=0)
    if sources > owners:
        tri += jnp.concatenate(
            [tri_ref[s, r].astype(jnp.float32) for s in range(owners, sources)], axis=0
        )
    tri_normed = norm_axis(tri, 0).astype(jnp.bfloat16)
    out = dot(tri_normed, wo_ref[u], ((0,), (0,)))
    gate = jax.nn.sigmoid(dot(normed, w_ref[u, :, 4 * width :], ((1,), (0,))))
    return (state_ref[r].astype(jnp.float32) + gate * out).astype(jnp.bfloat16)


def each_row(part, body):
    def row(r, carry):
        body(r)
        return carry

    lax.fori_loop(part[0], part[0] + part[1], row, 0)


def first_kernel(n, parts, state, pair_mask, token_mask, w, left, right, left_src, right_src, *sems):
    net = Net(n, True)
    swaps = [
        Swap(net, "half", left_src, left, sems[:3], parts),
        Swap(net, "both", right_src, right, sems[3:], parts),
    ]
    width = left.shape[0] * left.shape[2]
    net.greet()

    def body(r):
        normed = normed_row(state, r)
        mask = mask_row(pair_mask, token_mask, r)
        project_row(normed, w[0, :, : 2 * width], mask, left_src, r)
        project_row(normed, w[0, :, 2 * width : 4 * width], mask, right_src, r)

    for t in range(len(parts)):
        each_row(parts[t], body)
        if t == 0:
            net.met()
        send_rows(net, swaps, t)
    for swap in swaps:
        for t in range(len(parts)):
            swap.arrived(t)
        swap.sent()


def middle_kernel(
    n, parts, state, pair_mask, token_mask, w, wo, w_next, tri_src, after, sides, tri, sides_src, *sems
):
    net = Net(n, True)
    tri_swap = Swap(net, "half", tri_src, tri, sems[:3], parts)
    sides_swap = Swap(net, "all", sides_src, sides, sems[3:], parts)
    net.greet()
    net.met()
    for t in range(len(parts)):
        send_rows(net, [tri_swap], t)

    def body(r):
        after[r] = finish_row(state, 0, w, wo, tri, r)
        mask = mask_row(pair_mask, token_mask, r)
        project_row(normed_row(after, r), w_next[...], mask, sides_src, r)

    for t in range(len(parts)):
        tri_swap.arrived(t)
        each_row(parts[t], body)
        send_rows(net, [sides_swap], t)
    tri_swap.sent()
    for t in range(len(parts)):
        sides_swap.arrived(t)
    sides_swap.sent()


def last_kernel(n, parts, state, w, wo, tri_src, after, tri, *sems):
    net = Net(n, True)
    swap = Swap(net, "all", tri_src, tri, sems, parts)
    net.greet()
    net.met()
    for t in range(len(parts)):
        send_rows(net, [swap], t)

    def body(r):
        after[r] = finish_row(state, 1, w, wo, tri, r)

    for t in range(len(parts)):
        swap.arrived(t)
        each_row(parts[t], body)
    swap.sent()


def call(body, ident, n, parts, swaps, args, outs, scratch):
    vmem = pl.BlockSpec(memory_space=pltpu.VMEM)
    dma = pltpu.SemaphoreType.DMA
    return pl.pallas_call(
        functools.partial(body, n, parts),
        out_shape=[jax.ShapeDtypeStruct(shape, jnp.bfloat16) for shape in outs],
        in_specs=[vmem] * len(args),
        out_specs=[vmem] * len(outs),
        scratch_shapes=[pltpu.VMEM(shape, jnp.bfloat16) for shape in scratch]
        + [dma, dma((len(parts),)), dma((len(parts),))] * swaps,
        compiler_params=pltpu.CompilerParams(
            collective_id=ident, has_side_effects=True, vmem_limit_bytes=28 * 2**20
        ),
    )(*args)


def on_device(pair, pair_mask, token_mask, w, wo):
    rows, tokens, _ = pair.shape
    n = lax.axis_size("row")
    h = n // 2
    width = wo.shape[1]
    share, part = width // h, width // n
    cols = token_mask[None, :]
    near, full = (h, rows, share, tokens), (n, rows, share, tokens)
    packed, slim = (n, rows, 2 * part, tokens), (n, rows, part, tokens)
    w_next = w[1, :, : 4 * width].reshape(-1, 2, 2, n, part).transpose(0, 2, 3, 1, 4)
    w_next = w_next.reshape(-1, 4 * width)

    left, right = call(
        first_kernel, 1, n, cut(rows, FIRST), 2, (pair, pair_mask, cols, w), (near, full), (near, near)
    )
    left = left.reshape(h * rows, share, tokens)
    right = right.reshape(tokens, share, tokens)
    tri = jnp.einsum("ick,jck->icj", left, right, preferred_element_type=jnp.float32)
    tri = tri.astype(jnp.bfloat16).reshape(near)
    state, sides = call(
        middle_kernel,
        2,
        n,
        cut(rows, MIDDLE),
        2,
        (pair, pair_mask, cols, w, wo, w_next, tri),
        (pair.shape, packed),
        (near, packed),
    )
    sides = sides.reshape(tokens, 2 * part, tokens)
    tri = jnp.einsum(
        "kci,kcj->icj", sides[:, :part], sides[:, part:], preferred_element_type=jnp.float32
    )
    tri = tri.astype(jnp.bfloat16).reshape(slim)
    return call(
        last_kernel, 3, n, cut(rows, LAST), 1, (state, w, wo, tri), (pair.shape,), (slim,)
    )[0]


def solution(mesh):
    return jax.shard_map(
        on_device,
        mesh=mesh,
        in_specs=(
            P(("groups", "row"), None, None),
            P(("groups", "row"), None),
            P("groups"),
            P(),
            P(),
        ),
        out_specs=P(("groups", "row"), None, None),
        check_vma=False,
    )
```
